32 devices in a mesh: parts: 2 (over y), term: 4 (over z), blk: 4 (over x, core).
Axes of the slice: x: 2, y: 2, z: 4, core: 2. Of those that a mesh axis runs over, the one named last changes fastest.
Arguments:
- wavefunction: bfloat16 [8, 384, 384], P('parts', 'term'), parts along dimension 0
- left_operator_table: bfloat16 [64, 3, 384, 384], P(('parts', 'term', 'blk')), parts along dimension 0
- op_right: bfloat16 [64, 3, 384, 384], P(('parts', 'term', 'blk')), parts along dimension 0
- term_source: int32 [64, 3], P(('parts', 'term', 'blk')), parts along dimension 0, may hold values from 0 to 3, as said below
- term_target: int32 [64, 3], P(('parts', 'term', 'blk')), parts along dimension 0, may hold values from 0 to 3, as said below
Outputs:
- applied: float32 [8, 384, 384], P('parts', 'term'), parts along dimension 0
- residual: float32 [8, 384, 384], P('parts', 'term'), parts along dimension 0
The draws below stay inside these ranges and needn't reach their ends.
There are 2 independent parts, one for each index of `parts`. The reference program is written for one: setup_inputs(seed, part) draws one part's arguments, and reference() takes and returns one part's arrays. A program takes and returns all parts, laid end to end along the dimension named above; each array names one. Nothing has to cross between parts.
Inputs may be any that keep to these rules, and one draw needn't show every extreme that they name: Each term has one shift q in -1, 0, 1; term_target = term_source + q; the 3 sources of a term are distinct and increasing, and all targets are sectors. term_target[t,k] = term_source[t,k] + q of term t, the same q for all slots of a term.
All inputs are finite; a program needn't handle non-finite values.
Results may differ from the reference program's by a relative error of at most 0.0031.
Values may be sent and summed in bfloat16 or wider, within the bound.
A program may use at most 64 MiB of HBM per device.

```python
import jax
import jax.numpy as jnp
from jax import lax

SECTORS = 4
KSEC = 3
BLOCK = 384
TERMS = 32


def sector_lookup(key):
    shifts = jax.random.randint(jax.random.fold_in(key, 11), (TERMS,), -1, 2)
    dropped = jax.random.randint(jax.random.fold_in(key, 12), (TERMS,), 0, SECTORS)
    slots = jnp.arange(SECTORS - 1, dtype=jnp.int32)[None, :]
    skipped = slots + (slots >= dropped[:, None]).astype(jnp.int32)
    source = jnp.where(shifts[:, None] == 1, slots, jnp.where(shifts[:, None] == -1, slots + 1, skipped))
    target = source + shifts[:, None]
    return (source.astype(jnp.int32), target.astype(jnp.int32))


def operator_blocks(key):
    key_noise = jax.random.fold_in(key, 21)
    key_size = jax.random.fold_in(key, 22)
    key_sign = jax.random.fold_in(key, 23)
    shape = (TERMS, SECTORS - 1, BLOCK, BLOCK)
    noise_part = jax.random.normal(key_noise, shape, jnp.float32)
    diagonal_size = jnp.exp(jax.random.uniform(key_size, (TERMS, SECTORS - 1, BLOCK)) * 0.6931472)
    block_sign = jnp.where(jax.random.uniform(key_sign, (TERMS, SECTORS - 1, 1)) < 0.5, 1.0, -1.0)
    identity = jnp.eye(BLOCK, dtype=jnp.float32)
    diagonal_part = identity[None, None] * (diagonal_size * block_sign)[..., None]
    weighted_products = (noise_part / BLOCK ** 0.5 + diagonal_part) * TERMS ** (-0.25)
    return weighted_products.astype(jnp.bfloat16)


def draw_term_source(key, part):
    return sector_lookup(key)[0]


def draw_term_target(key, part):
    return sector_lookup(key)[1]


def draw_left_operator_table(key, part):
    key = jax.random.fold_in(key, 3)
    return operator_blocks(key)


def draw_op_right(key, part):
    key = jax.random.fold_in(key, 4)
    return operator_blocks(key)


def draw_wavefunction(key, part):
    key = jax.random.fold_in(key, 5)
    shape = (SECTORS, BLOCK, BLOCK)
    row_place = jnp.arange(BLOCK, dtype=jnp.float32) / (BLOCK - 1)
    row_scale = jnp.exp(row_place * 1.0986123)[None, :, None]
    row_scale = row_scale * 10.0 ** jax.random.uniform(jax.random.fold_in(key, 31), (SECTORS, BLOCK, 1))
    column_scale = 10.0 ** jax.random.uniform(jax.random.fold_in(key, 32), (SECTORS, 1, BLOCK))
    base_draw = jax.random.normal(jax.random.fold_in(key, 33), shape, jnp.float32)
    return (base_draw * row_scale * column_scale / 40.0).astype(jnp.bfloat16)


def setup_inputs(seed: int = 0, part: int = 0) -> dict:
    splits = jax.random.split(jax.random.key(seed), 6)
    own_keys = jax.random.split(jax.random.fold_in(splits[5], part), 6)
    return {
        "wavefunction": draw_wavefunction(jax.random.fold_in(jax.random.fold_in(splits[5], part), 71), part),
        "left_operator_table": draw_left_operator_table(jax.random.fold_in(jax.random.fold_in(splits[5], part), 71), part),
        "op_right": draw_op_right(jax.random.fold_in(jax.random.fold_in(splits[5], part), 71), part),
        "term_source": draw_term_source(jax.random.fold_in(jax.random.fold_in(splits[5], part), 71), part),
        "term_target": draw_term_target(jax.random.fold_in(jax.random.fold_in(splits[5], part), 71), part),
    }


def reference(wavefunction, left_operator_table, op_right, term_source, term_target):
    left_operator_blocks = left_operator_table.reshape(TERMS * KSEC, BLOCK, BLOCK)
    right_blocks = op_right.reshape(TERMS * KSEC, BLOCK, BLOCK)
    source = term_source.reshape(TERMS * KSEC).astype(jnp.int32)
    target = term_target.reshape(TERMS * KSEC).astype(jnp.int32)

    def add_term(running, term_record):
        left_block, right_block, from_sector, to_sector = term_record
        sector_block = lax.dynamic_index_in_dim(wavefunction, from_sector, 0, keepdims=False)
        half_product = jnp.dot(left_block, sector_block, preferred_element_type=jnp.float32).astype(jnp.bfloat16)
        contribution = jnp.dot(half_product, right_block.T, preferred_element_type=jnp.float32)
        updated = lax.dynamic_index_in_dim(running, to_sector, 0, keepdims=False) + contribution
        return lax.dynamic_update_index_in_dim(running, updated, to_sector, 0), None

    start_sum = jnp.zeros((SECTORS, BLOCK, BLOCK), jnp.float32)
    applied, _ = lax.scan(add_term, start_sum, (left_operator_blocks, right_blocks, source, target))
    wave_float = wavefunction.astype(jnp.float32)
    correlation = jnp.sum(wave_float * applied)
    norm_squared = jnp.sum(wave_float * wave_float)
    rayleigh = correlation / (norm_squared + 1e-6)
    residual = applied - rayleigh * wave_float
    return applied, residual
```

```python
import functools

import jax
import jax.numpy as jnp
from jax import lax
from jax.experimental import pallas as pl
from jax.experimental.pallas import tpu as pltpu
from jax.sharding import PartitionSpec as P

MESH = pl.DeviceIdType.MESH
F32 = jnp.float32
BF16 = jnp.bfloat16


def fold(product):
    rows, columns = product.shape
    return jnp.sum(product.reshape(rows // 8, 8, columns), axis=0)


def kernel(
    n, psi_ref, left_hbm, right_hbm, source_ref, target_ref,
    out_ref, rayleigh_ref,
    psi_all, left, right, half, kept, pair_send, pair_recv, x_send, x_recv, z_send, z_recv,
    own_block, dots, dots_recv,
    load_sem, gz_s, gz_r, gx_s, gx_r, gc_s, gc_r, gd_s, gd_r,
    pair_s, pair_r, x_s, x_r, z_s, z_r, out_s, out_r, dot_s, dot_r,
):
    terms, slots = left.shape[0], left.shape[1]
    rows = psi_ref.shape[1]
    me = lax.axis_index("term")
    blk = lax.axis_index("blk")
    core = lax.rem(blk, 2)
    x = lax.div(blk, 2)
    sib = blk + 1 - 2 * core
    across = blk + 2 - 4 * x
    diagonal = across + 1 - 2 * core

    loads = []
    for t in range(terms):
        loads.append(pltpu.make_async_copy(left_hbm.at[t], left.at[t], load_sem.at[0, t]))
        loads.append(pltpu.make_async_copy(right_hbm.at[t], right.at[t], load_sem.at[1, t]))
    for load in loads:
        load.start()

    def near(i):
        low = i + jnp.where(me <= i, 1, 0)
        high = n - 1 - (i + jnp.where(n - 1 - me <= i, 1, 0))
        return jnp.where(2 * me < n, low, high)

    peers = [near(i) for i in range(n - 1)]

    barrier = pltpu.get_barrier_semaphore()
    for peer in peers:
        pl.semaphore_signal(barrier, inc=1, device_id={"term": peer}, device_id_type=MESH)
    for peer in (sib, across, diagonal):
        pl.semaphore_signal(barrier, inc=1, device_id={"blk": peer}, device_id_type=MESH)
    pl.semaphore_wait(barrier, n - 1 + 3)

    sends = []

    def remote(src, dst, send, recv, where):
        return pltpu.make_async_remote_copy(
            src_ref=src, dst_ref=dst, send_sem=send, recv_sem=recv, device_id=where, device_id_type=MESH
        )

    def push(src, dst, send, recv, where):
        copy = remote(src, dst, send, recv, where)
        copy.start()
        sends.append(copy)

    def arrive(dst, send, recv, where):
        remote(dst, dst, send, recv, where).wait_recv()

    def span(z):
        return pl.ds(pl.multiple_of(z * rows, rows), rows)

    for peer in peers:
        push(psi_ref.at[blk], psi_all.at[blk, span(me)], gz_s.at[peer], gz_r.at[me], {"term": peer})
    for s in range(psi_ref.shape[0]):
        psi_all[s, span(me)] = psi_ref[s]

    for peer in peers:
        piece = psi_all.at[blk, span(peer)]
        arrive(piece, gz_s.at[peer], gz_r.at[peer], {"term": peer})
        push(piece, piece, gx_s.at[peer], gx_r.at[peer], {"blk": across})
        push(piece, piece, gc_s.at[peer], gc_r.at[peer], {"blk": sib})
    for peer in peers:
        piece = psi_all.at[across, span(peer)]
        arrive(piece, gx_s.at[peer], gx_r.at[peer], {"blk": across})
        push(piece, piece, gd_s.at[peer], gd_r.at[peer], {"blk": sib})
    for t in range(terms):
        half[t, slots] = jnp.zeros(half.shape[2:], BF16)
    for load in loads:
        load.wait()
    for peer in peers:
        arrive(psi_all.at[sib, span(peer)], gc_s.at[peer], gc_r.at[peer], {"blk": sib})
        arrive(psi_all.at[diagonal, span(peer)], gd_s.at[peer], gd_r.at[peer], {"blk": sib})

    for t in range(terms):
        for k in range(slots):
            half[t, k] = jnp.dot(
                left[t, k], psi_all[source_ref[t, k]], preferred_element_type=F32
            ).astype(BF16)

    def partial(s):
        total = None
        for t in range(terms):
            k = slots
            for slot in range(slots):
                k = jnp.where(target_ref[t, slot] == s, slot, k)
            product = lax.dot_general(
                half[t, k], right[t, jnp.minimum(k, slots - 1)],
                (((1,), (1,)), ((), ())), preferred_element_type=F32,
            )
            total = product if total is None else total + product
        return total, fold(psi_all[s].astype(F32) * total)

    far = peers[::-1]
    order = far + [me]

    value, dot = partial(diagonal)
    pair_send[0] = value.astype(BF16)
    push(pair_send.at[0], pair_recv.at[0], pair_s.at[0], pair_r.at[0], {"blk": sib})
    value, more = partial(across)
    dot = dot + more
    kept[0] = value
    arrive(pair_recv.at[0], pair_s.at[0], pair_r.at[0], {"blk": sib})
    for z in order:
        x_send[span(z)] = (kept[0, span(z)] + pair_recv[0, span(z)].astype(F32)).astype(BF16)
        push(x_send.at[span(z)], x_recv.at[span(z)], x_s.at[z], x_r.at[z], {"blk": across})
    value, more = partial(sib)
    dot = dot + more
    pair_send[1] = value.astype(BF16)
    push(pair_send.at[1], pair_recv.at[1], pair_s.at[1], pair_r.at[1], {"blk": sib})
    value, more = partial(blk)
    dots[0] = dot + more
    push(dots.at[0], dots_recv.at[0], dot_s.at[0], dot_r.at[0], {"blk": sib})
    kept[1] = value
    arrive(pair_recv.at[1], pair_s.at[1], pair_r.at[1], {"blk": sib})

    for i, z in enumerate(order):
        arrive(x_recv.at[span(z)], x_s.at[z], x_r.at[z], {"blk": across})
        block = (kept[1, span(z)] + pair_recv[1, span(z)].astype(F32)) + x_recv[span(z)].astype(F32)
        if i < n - 1:
            z_send[i] = block.astype(BF16)
            push(z_send.at[i], z_recv.at[me], z_s.at[z], z_r.at[me], {"term": z})
        else:
            own_block[...] = block
        if i == 0:
            arrive(dots_recv.at[0], dot_s.at[0], dot_r.at[0], {"blk": sib})
            dots[1] = dots[0] + dots_recv[0]
            push(dots.at[1], dots_recv.at[1], dot_s.at[1], dot_r.at[1], {"blk": across})
        if i == 2:
            arrive(dots_recv.at[1], dot_s.at[1], dot_r.at[1], {"blk": across})
            dots[2] = dots[1] + dots_recv[1]
            for peer in peers:
                push(dots.at[2], dots_recv.at[2 + me], dot_s.at[2 + peer], dot_r.at[2 + me], {"term": peer})

    norm = None
    for s in range(psi_ref.shape[0]):
        wave = psi_all[s].astype(F32)
        norm = fold(wave * wave) if norm is None else norm + fold(wave * wave)
    norm_squared = jnp.sum(norm)

    total = own_block[...]
    for peer in peers:
        arrive(z_recv.at[peer], z_s.at[peer], z_r.at[peer], {"term": peer})
        total = total + z_recv[peer].astype(F32)
    out_ref[blk] = total.astype(BF16)
    for i, peer in enumerate((across, diagonal, sib)):
        push(out_ref.at[blk], out_ref.at[blk], out_s.at[i], out_r.at[i], {"blk": peer})

    for peer in peers:
        arrive(dots_recv.at[2 + peer], dot_s.at[2 + peer], dot_r.at[2 + peer], {"term": peer})
    dots_recv[2 + me] = dots[2]
    correlation = dots_recv[2]
    for z in range(1, n):
        correlation = correlation + dots_recv[2 + z]
    rayleigh_ref[...] = jnp.full(
        rayleigh_ref.shape, jnp.sum(correlation) / (norm_squared + 1e-06), F32
    )
    for i, peer in enumerate((across, diagonal, sib)):
        arrive(out_ref.at[peer], out_s.at[i], out_r.at[i], {"blk": peer})
    for copy in sends:
        copy.wait_send()


def fused(wavefunction, left_operator_table, op_right, term_source, term_target, n):
    sectors, rows, width = wavefunction.shape
    terms, slots = left_operator_table.shape[:2]
    block = (width, width)
    dma = pltpu.SemaphoreType.DMA
    vmem = pl.BlockSpec(memory_space=pltpu.VMEM)
    smem = pl.BlockSpec(memory_space=pltpu.SMEM)
    hbm = pl.BlockSpec(memory_space=pl.ANY)
    out, rayleigh = pl.pallas_call(
        functools.partial(kernel, n),
        out_shape=(
            jax.ShapeDtypeStruct((sectors, rows, width), BF16),
            jax.ShapeDtypeStruct((8, 128), F32),
        ),
        in_specs=[vmem, hbm, hbm, smem, smem],
        out_specs=(vmem, vmem),
        scratch_shapes=[
            pltpu.VMEM((sectors,) + block, BF16),
            pltpu.VMEM((terms, slots) + block, BF16),
            pltpu.VMEM((terms, slots) + block, BF16),
            pltpu.VMEM((terms, slots + 1) + block, BF16),
            pltpu.VMEM((2,) + block, F32),
            pltpu.VMEM((2,) + block, BF16),
            pltpu.VMEM((2,) + block, BF16),
            pltpu.VMEM(block, BF16),
            pltpu.VMEM(block, BF16),
            pltpu.VMEM((n - 1, rows, width), BF16),
            pltpu.VMEM((n, rows, width), BF16),
            pltpu.VMEM((rows, width), F32),
            pltpu.VMEM((3, 8, width), F32),
            pltpu.VMEM((2 + n, 8, width), F32),
            dma((2, terms)),
            dma((n,)), dma((n,)), dma((n,)), dma((n,)), dma((n,)), dma((n,)), dma((n,)), dma((n,)),
            dma((2,)), dma((2,)), dma((n,)), dma((n,)), dma((n,)), dma((n,)),
            dma((3,)), dma((3,)), dma((2 + n,)), dma((2 + n,)),
        ],
        compiler_params=pltpu.CompilerParams(
            collective_id=0, has_side_effects=True, vmem_limit_bytes=48 * 1024 * 1024
        ),
    )(wavefunction, left_operator_table, op_right, term_source, term_target)
    applied = out.astype(F32)
    return applied, applied - rayleigh[0, 0] * wavefunction.astype(F32)


def plain(wavefunction, left_operator_table, op_right, term_source, term_target):
    sectors = wavefunction.shape[0]
    block_width = wavefunction.shape[2]
    item_count = left_operator_table.shape[0] * left_operator_table.shape[1]
    left_operator_blocks = left_operator_table.reshape(item_count, block_width, block_width)
    right_blocks = op_right.reshape(item_count, block_width, block_width)
    source = term_source.reshape(item_count)
    target = term_target.reshape(item_count)
    whole_psi = lax.all_gather(wavefunction, "term", axis=1, tiled=True)
    selected_blocks = jnp.take(whole_psi, source, axis=0)
    half_products = jnp.einsum(
        "xwm,xmp->xwp", left_operator_blocks, selected_blocks, preferred_element_type=F32
    )
    half_products = half_products.astype(BF16)
    term_products = jnp.einsum(
        "iab,icb->iac", half_products, right_blocks, preferred_element_type=F32
    )
    onehot = (target[:, None] == jnp.arange(sectors, dtype=jnp.int32)[None, :]).astype(F32)
    partial_value = jnp.einsum(
        "is,iac->sac", onehot, term_products, precision=lax.Precision.HIGHEST
    )
    column_share = lax.psum_scatter(partial_value, "blk", scatter_dimension=2, tiled=True)
    both_share = lax.psum_scatter(column_share, "term", scatter_dimension=1, tiled=True)
    applied = lax.all_gather(both_share, "blk", axis=2, tiled=True)
    wave_float = wavefunction.astype(F32)
    correlation, norm_squared = lax.psum(
        (jnp.sum(wave_float * applied), jnp.sum(wave_float * wave_float)), "term"
    )
    rayleigh = correlation / (norm_squared + 1e-06)
    residual = applied - rayleigh * wave_float
    return (applied, residual)


def solution(mesh):
    n, groups = mesh.shape["term"], mesh.shape["blk"]

    def local(wavefunction, *rest):
        sectors, rows, _ = wavefunction.shape
        if groups == sectors == 4 and n == 4 and rows % 16 == 0:
            return fused(wavefunction, *rest, n)
        return plain(wavefunction, *rest)

    return jax.shard_map(
        local,
        mesh=mesh,
        in_specs=(
            P("parts", "term", None),
            P(("parts", "term", "blk"), None, None, None),
            P(("parts", "term", "blk"), None, None, None),
            P(("parts", "term", "blk"), None),
            P(("parts", "term", "blk"), None),
        ),
        out_specs=(P("parts", "term", None), P("parts", "term", None)),
        check_vma=False,
    )
```

```python
import functools

import jax
import jax.numpy as jnp
from jax import lax
from jax.experimental import pallas as pl
from jax.experimental.pallas import tpu as pltpu
from jax.sharding import PartitionSpec as P

MESH = pl.DeviceIdType.MESH
F32 = jnp.float32
BF16 = jnp.bfloat16


def fold(product):
    rows, columns = product.shape
    return jnp.sum(product.reshape(rows // 8, 8, columns), axis=0)


def kernel(
    n, psi_ref, left_hbm, right_hbm, source_ref, target_ref,
    out_ref, rayleigh_ref,
    psi_all, left, right, half, kept, pair_send, pair_recv, x_send, x_recv, z_send, z_recv,
    own_block, dots, dots_recv,
    own_sem, load_sem, gz_s, gz_r, gx_s, gx_r, gc_s, gc_r,
    pair_s, pair_r, x_s, x_r, z_s, z_r, out_s, out_r, dot_s, dot_r,
):
    terms, slots = left.shape[0], left.shape[1]
    rows = psi_ref.shape[1]
    me = lax.axis_index("term")
    blk = lax.axis_index("blk")
    core = lax.rem(blk, 2)
    x = lax.div(blk, 2)
    sib = blk + 1 - 2 * core
    across = blk + 2 - 4 * x
    diagonal = across + 1 - 2 * core

    loads = []
    for t in range(terms):
        loads.append(pltpu.make_async_copy(left_hbm.at[t], left.at[t], load_sem.at[0, t]))
        loads.append(pltpu.make_async_copy(right_hbm.at[t], right.at[t], load_sem.at[1, t]))
    own_rows = pltpu.make_async_copy(psi_ref, psi_all.at[:, pl.ds(pl.multiple_of(me * rows, rows), rows)], own_sem)
    own_rows.start()
    for load in loads:
        load.start()

    def near(i):
        low = i + jnp.where(me <= i, 1, 0)
        high = n - 1 - (i + jnp.where(n - 1 - me <= i, 1, 0))
        return jnp.where(2 * me < n, low, high)

    peers = [near(i) for i in range(n - 1)]

    barrier = pltpu.get_barrier_semaphore()
    for peer in peers:
        pl.semaphore_signal(barrier, inc=1, device_id={"term": peer}, device_id_type=MESH)
    for peer in (sib, across, diagonal):
        pl.semaphore_signal(barrier, inc=1, device_id={"blk": peer}, device_id_type=MESH)
    pl.semaphore_wait(barrier, n - 1 + 3)

    sends = []

    def remote(src, dst, send, recv, where):
        return pltpu.make_async_remote_copy(
            src_ref=src, dst_ref=dst, send_sem=send, recv_sem=recv, device_id=where, device_id_type=MESH
        )

    def push(src, dst, send, recv, where):
        copy = remote(src, dst, send, recv, where)
        copy.start()
        sends.append(copy)

    def arrive(dst, send, recv, where):
        remote(dst, dst, send, recv, where).wait_recv()

    def span(z):
        return pl.ds(pl.multiple_of(z * rows, rows), rows)

    crossing = rows * 2 // 3 // 16 * 16

    def upper(z):
        return pl.ds(pl.multiple_of(z * rows, 16), crossing)

    def lower(z):
        return pl.ds(pl.multiple_of(z * rows + crossing, 16), rows - crossing)

    def straight():
        for peer in peers:
            for i, s in enumerate((blk, across)):
                push(psi_ref.at[s, pl.ds(crossing, rows - crossing)], psi_all.at[s, lower(me)],
                     gz_s.at[1 + i, peer], gz_r.at[1 + i, me], {"term": peer})

    for peer in peers:
        push(psi_ref.at[blk, pl.ds(0, crossing)], psi_all.at[blk, upper(me)],
             gz_s.at[0, peer], gz_r.at[0, me], {"term": peer})
    for i, peer in enumerate(peers):
        piece = psi_all.at[blk, upper(peer)]
        arrive(piece, gz_s.at[0, peer], gz_r.at[0, peer], {"term": peer})
        push(piece, piece, gx_s.at[peer], gx_r.at[peer], {"blk": across})
        if i == 0:
            straight()
        push(piece, piece, gc_s.at[0, peer], gc_r.at[0, peer], {"blk": sib})
    for peer in peers:
        for i, s in enumerate((blk, across)):
            piece = psi_all.at[s, lower(peer)]
            arrive(piece, gz_s.at[1 + i, peer], gz_r.at[1 + i, peer], {"term": peer})
            push(piece, piece, gc_s.at[1 + i, peer], gc_r.at[1 + i, peer], {"blk": sib})
    for peer in peers:
        piece = psi_all.at[across, upper(peer)]
        arrive(piece, gx_s.at[peer], gx_r.at[peer], {"blk": across})
        push(piece, piece, gc_s.at[3, peer], gc_r.at[3, peer], {"blk": sib})
    for t in range(terms):
        half[t, slots] = jnp.zeros(half.shape[2:], BF16)
    own_rows.wait()
    for load in loads:
        load.wait()
    for peer in peers:
        for i, piece in enumerate((
            psi_all.at[sib, upper(peer)], psi_all.at[sib, lower(peer)],
            psi_all.at[diagonal, lower(peer)], psi_all.at[diagonal, upper(peer)],
        )):
            arrive(piece, gc_s.at[i, peer], gc_r.at[i, peer], {"blk": sib})

    for t in range(terms):
        for k in range(slots):
            half[t, k] = jnp.dot(
                left[t, k], psi_all[source_ref[t, k]], preferred_element_type=F32
            ).astype(BF16)

    def partial(s):
        total = None
        for t in range(terms):
            k = slots
            for slot in range(slots):
                k = jnp.where(target_ref[t, slot] == s, slot, k)
            product = lax.dot_general(
                half[t, k], right[t, jnp.minimum(k, slots - 1)],
                (((1,), (1,)), ((), ())), preferred_element_type=F32,
            )
            total = product if total is None else total + product
        return total, fold(psi_all[s].astype(F32) * total)

    far = peers[::-1]
    order = far + [me]

    value, dot = partial(diagonal)
    pair_send[0] = value.astype(BF16)
    push(pair_send.at[0], pair_recv.at[0], pair_s.at[0], pair_r.at[0], {"blk": sib})
    value, more = partial(across)
    dot = dot + more
    kept[0] = value
    arrive(pair_recv.at[0], pair_s.at[0], pair_r.at[0], {"blk": sib})
    for z in order:
        x_send[span(z)] = (kept[0, span(z)] + pair_recv[0, span(z)].astype(F32)).astype(BF16)
        push(x_send.at[span(z)], x_recv.at[span(z)], x_s.at[z], x_r.at[z], {"blk": across})
    value, more = partial(sib)
    dot = dot + more
    pair_send[1] = value.astype(BF16)
    push(pair_send.at[1], pair_recv.at[1], pair_s.at[1], pair_r.at[1], {"blk": sib})
    value, more = partial(blk)
    dots[0] = dot + more
    push(dots.at[0], dots_recv.at[0], dot_s.at[0], dot_r.at[0], {"blk": sib})
    kept[1] = value
    arrive(pair_recv.at[1], pair_s.at[1], pair_r.at[1], {"blk": sib})

    for i, z in enumerate(order):
        arrive(x_recv.at[span(z)], x_s.at[z], x_r.at[z], {"blk": across})
        block = (kept[1, span(z)] + pair_recv[1, span(z)].astype(F32)) + x_recv[span(z)].astype(F32)
        if i < n - 1:
            z_send[i] = block.astype(BF16)
            push(z_send.at[i], z_recv.at[me], z_s.at[z], z_r.at[me], {"term": z})
        else:
            own_block[...] = block
        if i == 0:
            arrive(dots_recv.at[0], dot_s.at[0], dot_r.at[0], {"blk": sib})
            dots[1] = dots[0] + dots_recv[0]
            push(dots.at[1], dots_recv.at[1], dot_s.at[1], dot_r.at[1], {"blk": across})
        if i == 2:
            arrive(dots_recv.at[1], dot_s.at[1], dot_r.at[1], {"blk": across})
            dots[2] = dots[1] + dots_recv[1]
            for peer in peers:
                push(dots.at[2], dots_recv.at[2 + me], dot_s.at[2 + peer], dot_r.at[2 + me], {"term": peer})

    norm = None
    for s in range(psi_ref.shape[0]):
        wave = psi_all[s].astype(F32)
        norm = fold(wave * wave) if norm is None else norm + fold(wave * wave)
    norm_squared = jnp.sum(norm)

    total = own_block[...]
    for peer in peers:
        arrive(z_recv.at[peer], z_s.at[peer], z_r.at[peer], {"term": peer})
        total = total + z_recv[peer].astype(F32)
    out_ref[blk] = total.astype(BF16)
    for i, peer in enumerate((across, diagonal, sib)):
        push(out_ref.at[blk], out_ref.at[blk], out_s.at[i], out_r.at[i], {"blk": peer})

    for peer in peers:
        arrive(dots_recv.at[2 + peer], dot_s.at[2 + peer], dot_r.at[2 + peer], {"term": peer})
    dots_recv[2 + me] = dots[2]
    correlation = dots_recv[2]
    for z in range(1, n):
        correlation = correlation + dots_recv[2 + z]
    rayleigh_ref[...] = jnp.full(
        rayleigh_ref.shape, jnp.sum(correlation) / (norm_squared + 1e-06), F32
    )
    for i, peer in enumerate((across, diagonal, sib)):
        arrive(out_ref.at[peer], out_s.at[i], out_r.at[i], {"blk": peer})
    for copy in sends:
        copy.wait_send()


def fused(wavefunction, left_operator_table, op_right, term_source, term_target, n):
    sectors, rows, width = wavefunction.shape
    terms, slots = left_operator_table.shape[:2]
    block = (width, width)
    dma = pltpu.SemaphoreType.DMA
    vmem = pl.BlockSpec(memory_space=pltpu.VMEM)
    smem = pl.BlockSpec(memory_space=pltpu.SMEM)
    hbm = pl.BlockSpec(memory_space=pl.ANY)
    out, rayleigh = pl.pallas_call(
        functools.partial(kernel, n),
        out_shape=(
            jax.ShapeDtypeStruct((sectors, rows, width), BF16),
            jax.ShapeDtypeStruct((rows, width), F32),
        ),
        in_specs=[hbm, hbm, hbm, smem, smem],
        out_specs=(vmem, vmem),
        scratch_shapes=[
            pltpu.VMEM((sectors,) + block, BF16),
            pltpu.VMEM((terms, slots) + block, BF16),
            pltpu.VMEM((terms, slots) + block, BF16),
            pltpu.VMEM((terms, slots + 1) + block, BF16),
            pltpu.VMEM((2,) + block, F32),
            pltpu.VMEM((2,) + block, BF16),
            pltpu.VMEM((2,) + block, BF16),
            pltpu.VMEM(block, BF16),
            pltpu.VMEM(block, BF16),
            pltpu.VMEM((n - 1, rows, width), BF16),
            pltpu.VMEM((n, rows, width), BF16),
            pltpu.VMEM((rows, width), F32),
            pltpu.VMEM((3, 8, width), F32),
            pltpu.VMEM((2 + n, 8, width), F32),
            dma, dma((2, terms)),
            dma((3, n)), dma((3, n)), dma((n,)), dma((n,)), dma((4, n)), dma((4, n)),
            dma((2,)), dma((2,)), dma((n,)), dma((n,)), dma((n,)), dma((n,)),
            dma((3,)), dma((3,)), dma((2 + n,)), dma((2 + n,)),
        ],
        compiler_params=pltpu.CompilerParams(
            collective_id=0, has_side_effects=True, vmem_limit_bytes=60 * 1024 * 1024
        ),
    )(wavefunction, left_operator_table, op_right, term_source, term_target)
    applied = out.astype(F32)
    return applied, applied - rayleigh * wavefunction.astype(F32)


def plain(wavefunction, left_operator_table, op_right, term_source, term_target):
    sectors = wavefunction.shape[0]
    block_width = wavefunction.shape[2]
    item_count = left_operator_table.shape[0] * left_operator_table.shape[1]
    left_operator_blocks = left_operator_table.reshape(item_count, block_width, block_width)
    right_blocks = op_right.reshape(item_count, block_width, block_width)
    source = term_source.reshape(item_count)
    target = term_target.reshape(item_count)
    whole_psi = lax.all_gather(wavefunction, "term", axis=1, tiled=True)
    selected_blocks = jnp.take(whole_psi, source, axis=0)
    half_products = jnp.einsum(
        "xwm,xmp->xwp", left_operator_blocks, selected_blocks, preferred_element_type=F32
    )
    half_products = half_products.astype(BF16)
    term_products = jnp.einsum(
        "iab,icb->iac", half_products, right_blocks, preferred_element_type=F32
    )
    onehot = (target[:, None] == jnp.arange(sectors, dtype=jnp.int32)[None, :]).astype(F32)
    partial_value = jnp.einsum(
        "is,iac->sac", onehot, term_products, precision=lax.Precision.HIGHEST
    )
    column_share = lax.psum_scatter(partial_value, "blk", scatter_dimension=2, tiled=True)
    both_share = lax.psum_scatter(column_share, "term", scatter_dimension=1, tiled=True)
    applied = lax.all_gather(both_share, "blk", axis=2, tiled=True)
    wave_float = wavefunction.astype(F32)
    correlation, norm_squared = lax.psum(
        (jnp.sum(wave_float * applied), jnp.sum(wave_float * wave_float)), "term"
    )
    rayleigh = correlation / (norm_squared + 1e-06)
    residual = applied - rayleigh * wave_float
    return (applied, residual)


def solution(mesh):
    n, groups = mesh.shape["term"], mesh.shape["blk"]

    def local(wavefunction, *rest):
        sectors, rows, _ = wavefunction.shape
        if groups == sectors == 4 and n == 4 and rows % 16 == 0:
            return fused(wavefunction, *rest, n)
        return plain(wavefunction, *rest)

    return jax.shard_map(
        local,
        mesh=mesh,
        in_specs=(
            P("parts", "term", None),
            P(("parts", "term", "blk"), None, None, None),
            P(("parts", "term", "blk"), None, None, None),
            P(("parts", "term", "blk"), None),
            P(("parts", "term", "blk"), None),
        ),
        out_specs=(P("parts", "term", None), P("parts", "term", None)),
        check_vma=False,
    )
```

```python
import functools

import jax
import jax.numpy as jnp
from jax import lax
from jax.experimental import pallas as pl
from jax.experimental.pallas import tpu as pltpu
from jax.sharding import PartitionSpec as P

MESH = pl.DeviceIdType.MESH
F32 = jnp.float32
BF16 = jnp.bfloat16


def fold(product):
    rows, columns = product.shape
    return jnp.sum(product.reshape(rows // 8, 8, columns), axis=0)


def kernel(
    n, psi_ref, left_hbm, right_hbm, source_ref, target_ref,
    out_ref, rayleigh_ref,
    psi_all, left, right, half, kept, pair_send, pair_recv, x_send, x_recv, z_send, z_recv,
    own_block, dots, dots_recv,
    own_sem, load_sem, gz_s, gz_r, gx_s, gx_r, gc_s, gc_r,
    pair_s, pair_r, x_s, x_r, z_s, z_r, out_s, out_r, dot_s, dot_r,
):
    terms, slots = left.shape[0], left.shape[1]
    rows = psi_ref.shape[1]
    me = lax.axis_index("term")
    blk = lax.axis_index("blk")
    core = lax.rem(blk, 2)
    x = lax.div(blk, 2)
    sib = blk + 1 - 2 * core
    across = blk + 2 - 4 * x
    diagonal = across + 1 - 2 * core

    loads = []
    for t in range(terms):
        loads.append(pltpu.make_async_copy(left_hbm.at[t], left.at[t], load_sem.at[0, t]))
        loads.append(pltpu.make_async_copy(right_hbm.at[t], right.at[t], load_sem.at[1, t]))
    own_rows = pltpu.make_async_copy(psi_ref, psi_all.at[:, pl.ds(pl.multiple_of(me * rows, rows), rows)], own_sem)
    own_rows.start()
    for load in loads:
        load.start()

    def near(i):
        low = i + jnp.where(me <= i, 1, 0)
        high = n - 1 - (i + jnp.where(n - 1 - me <= i, 1, 0))
        return jnp.where(2 * me < n, low, high)

    peers = [near(i) for i in range(n - 1)]

    barrier = pltpu.get_barrier_semaphore()
    for peer in peers:
        pl.semaphore_signal(barrier, inc=1, device_id={"term": peer}, device_id_type=MESH)
    for peer in (sib, across, diagonal):
        pl.semaphore_signal(barrier, inc=1, device_id={"blk": peer}, device_id_type=MESH)
    pl.semaphore_wait(barrier, n - 1 + 3)

    sends = []

    def remote(src, dst, send, recv, where):
        return pltpu.make_async_remote_copy(
            src_ref=src, dst_ref=dst, send_sem=send, recv_sem=recv, device_id=where, device_id_type=MESH
        )

    def push(src, dst, send, recv, where):
        copy = remote(src, dst, send, recv, where)
        copy.start()
        sends.append(copy)

    def arrive(dst, send, recv, where):
        remote(dst, dst, send, recv, where).wait_recv()

    def span(z):
        return pl.ds(pl.multiple_of(z * rows, rows), rows)

    crossing = rows * 2 // 3 // 16 * 16

    def upper(z):
        return pl.ds(pl.multiple_of(z * rows, 16), crossing)

    def lower(z):
        return pl.ds(pl.multiple_of(z * rows + crossing, 16), rows - crossing)

    def straight():
        for peer in peers:
            for i, s in enumerate((blk, across)):
                push(psi_ref.at[s, pl.ds(crossing, rows - crossing)], psi_all.at[s, lower(me)],
                     gz_s.at[1 + i, peer], gz_r.at[1 + i, me], {"term": peer})

    for peer in peers:
        push(psi_ref.at[blk, pl.ds(0, crossing)], psi_all.at[blk, upper(me)],
             gz_s.at[0, peer], gz_r.at[0, me], {"term": peer})
    for i, peer in enumerate(peers):
        piece = psi_all.at[blk, upper(peer)]
        arrive(piece, gz_s.at[0, peer], gz_r.at[0, peer], {"term": peer})
        push(piece, piece, gx_s.at[peer], gx_r.at[peer], {"blk": across})
        if i == 0:
            straight()
        push(piece, piece, gc_s.at[0, peer], gc_r.at[0, peer], {"blk": sib})
    for peer in peers:
        for i, s in enumerate((blk, across)):
            piece = psi_all.at[s, lower(peer)]
            arrive(piece, gz_s.at[1 + i, peer], gz_r.at[1 + i, peer], {"term": peer})
            push(piece, piece, gc_s.at[1 + i, peer], gc_r.at[1 + i, peer], {"blk": sib})
    for peer in peers:
        piece = psi_all.at[across, upper(peer)]
        arrive(piece, gx_s.at[peer], gx_r.at[peer], {"blk": across})
        push(piece, piece, gc_s.at[3, peer], gc_r.at[3, peer], {"blk": sib})
    for t in range(terms):
        half[t, slots] = jnp.zeros(half.shape[2:], BF16)
    own_rows.wait()
    for load in loads:
        load.wait()
    for peer in peers:
        for i, piece in enumerate((
            psi_all.at[sib, upper(peer)], psi_all.at[sib, lower(peer)],
            psi_all.at[diagonal, lower(peer)], psi_all.at[diagonal, upper(peer)],
        )):
            arrive(piece, gc_s.at[i, peer], gc_r.at[i, peer], {"blk": sib})

    for t in range(terms):
        for k in range(slots):
            half[t, k] = jnp.dot(
                left[t, k], psi_all[source_ref[t, k]], preferred_element_type=F32
            ).astype(BF16)

    width = psi_ref.shape[2]
    middle = width // 2 // 16 * 16

    def partial(s, low=0, high=width):
        total = None
        for t in range(terms):
            k = slots
            for slot in range(slots):
                k = jnp.where(target_ref[t, slot] == s, slot, k)
            product = lax.dot_general(
                half[t, k, low:high], right[t, jnp.minimum(k, slots - 1)],
                (((1,), (1,)), ((), ())), preferred_element_type=F32,
            )
            total = product if total is None else total + product
        return total

    far = peers[::-1]
    order = far + [me]

    def cross(z):
        x_send[span(z)] = (kept[0, span(z)] + pair_recv[0, span(z)].astype(F32)).astype(BF16)
        push(x_send.at[span(z)], x_recv.at[span(z)], x_s.at[z], x_r.at[z], {"blk": across})

    cuts = ((0, 0, middle), (2, middle, width))
    for i, low, high in cuts:
        value = partial(diagonal, low, high)
        pair_send[0, low:high] = value.astype(BF16)
        piece = pl.ds(low, high - low)
        push(pair_send.at[0, piece], pair_recv.at[0, piece], pair_s.at[i], pair_r.at[i], {"blk": sib})
        kept[2, low:high] = value
    kept[0] = partial(across)
    for i, low, high in cuts:
        arrive(pair_recv.at[0, pl.ds(low, high - low)], pair_s.at[i], pair_r.at[i], {"blk": sib})
    for z in order[:2]:
        cross(z)
    value = partial(sib)
    pair_send[1] = value.astype(BF16)
    push(pair_send.at[1], pair_recv.at[1], pair_s.at[1], pair_r.at[1], {"blk": sib})
    kept[3] = value
    for z in order[2:3]:
        cross(z)
    kept[1] = partial(blk)
    for z in order[3:4]:
        cross(z)
    dot = fold(psi_all[diagonal].astype(F32) * kept[2])
    for i, s in ((0, across), (3, sib), (1, blk)):
        dot = dot + fold(psi_all[s].astype(F32) * kept[i])
    for z in order[4:]:
        cross(z)
    dots[0] = dot
    push(dots.at[0], dots_recv.at[0], dot_s.at[0], dot_r.at[0], {"blk": sib})
    arrive(pair_recv.at[1], pair_s.at[1], pair_r.at[1], {"blk": sib})

    for i, z in enumerate(order):
        arrive(x_recv.at[span(z)], x_s.at[z], x_r.at[z], {"blk": across})
        block = (kept[1, span(z)] + pair_recv[1, span(z)].astype(F32)) + x_recv[span(z)].astype(F32)
        if i < n - 1:
            z_send[i] = block.astype(BF16)
            push(z_send.at[i], z_recv.at[me], z_s.at[z], z_r.at[me], {"term": z})
        else:
            own_block[...] = block
        if i == 0:
            arrive(dots_recv.at[0], dot_s.at[0], dot_r.at[0], {"blk": sib})
            dots[1] = dots[0] + dots_recv[0]
            push(dots.at[1], dots_recv.at[1], dot_s.at[1], dot_r.at[1], {"blk": across})
        if i == 2:
            arrive(dots_recv.at[1], dot_s.at[1], dot_r.at[1], {"blk": across})
            dots[2] = dots[1] + dots_recv[1]
            for peer in peers:
                push(dots.at[2], dots_recv.at[2 + me], dot_s.at[2 + peer], dot_r.at[2 + me], {"term": peer})

    norm = None
    for s in range(psi_ref.shape[0]):
        wave = psi_all[s].astype(F32)
        norm = fold(wave * wave) if norm is None else norm + fold(wave * wave)
    norm_squared = jnp.sum(norm)

    total = own_block[...]
    for peer in peers:
        arrive(z_recv.at[peer], z_s.at[peer], z_r.at[peer], {"term": peer})
        total = total + z_recv[peer].astype(F32)
    out_ref[blk] = total.astype(BF16)
    for i, peer in enumerate((across, diagonal, sib)):
        push(out_ref.at[blk], out_ref.at[blk], out_s.at[i], out_r.at[i], {"blk": peer})

    for peer in peers:
        arrive(dots_recv.at[2 + peer], dot_s.at[2 + peer], dot_r.at[2 + peer], {"term": peer})
    dots_recv[2 + me] = dots[2]
    correlation = dots_recv[2]
    for z in range(1, n):
        correlation = correlation + dots_recv[2 + z]
    rayleigh_ref[...] = jnp.full(
        rayleigh_ref.shape, jnp.sum(correlation) / (norm_squared + 1e-06), F32
    )
    for i, peer in enumerate((across, diagonal, sib)):
        arrive(out_ref.at[peer], out_s.at[i], out_r.at[i], {"blk": peer})
    for copy in sends:
        copy.wait_send()


def fused(wavefunction, left_operator_table, op_right, term_source, term_target, n):
    sectors, rows, width = wavefunction.shape
    terms, slots = left_operator_table.shape[:2]
    block = (width, width)
    dma = pltpu.SemaphoreType.DMA
    vmem = pl.BlockSpec(memory_space=pltpu.VMEM)
    smem = pl.BlockSpec(memory_space=pltpu.SMEM)
    hbm = pl.BlockSpec(memory_space=pl.ANY)
    out, rayleigh = pl.pallas_call(
        functools.partial(kernel, n),
        out_shape=(
            jax.ShapeDtypeStruct((sectors, rows, width), BF16),
            jax.ShapeDtypeStruct((rows, width), F32),
        ),
        in_specs=[hbm, hbm, hbm, smem, smem],
        out_specs=(vmem, vmem),
        scratch_shapes=[
            pltpu.VMEM((sectors,) + block, BF16),
            pltpu.VMEM((terms, slots) + block, BF16),
            pltpu.VMEM((terms, slots) + block, BF16),
            pltpu.VMEM((terms, slots + 1) + block, BF16),
            pltpu.VMEM((4,) + block, F32),
            pltpu.VMEM((2,) + block, BF16),
            pltpu.VMEM((2,) + block, BF16),
            pltpu.VMEM(block, BF16),
            pltpu.VMEM(block, BF16),
            pltpu.VMEM((n - 1, rows, width), BF16),
            pltpu.VMEM((n, rows, width), BF16),
            pltpu.VMEM((rows, width), F32),
            pltpu.VMEM((3, 8, width), F32),
            pltpu.VMEM((2 + n, 8, width), F32),
            dma, dma((2, terms)),
            dma((3, n)), dma((3, n)), dma((n,)), dma((n,)), dma((4, n)), dma((4, n)),
            dma((3,)), dma((3,)), dma((n,)), dma((n,)), dma((n,)), dma((n,)),
            dma((3,)), dma((3,)), dma((2 + n,)), dma((2 + n,)),
        ],
        compiler_params=pltpu.CompilerParams(
            collective_id=0, has_side_effects=True, vmem_limit_bytes=60 * 1024 * 1024
        ),
    )(wavefunction, left_operator_table, op_right, term_source, term_target)
    applied = out.astype(F32)
    return applied, applied - rayleigh * wavefunction.astype(F32)


def plain(wavefunction, left_operator_table, op_right, term_source, term_target):
    sectors = wavefunction.shape[0]
    block_width = wavefunction.shape[2]
    item_count = left_operator_table.shape[0] * left_operator_table.shape[1]
    left_operator_blocks = left_operator_table.reshape(item_count, block_width, block_width)
    right_blocks = op_right.reshape(item_count, block_width, block_width)
    source = term_source.reshape(item_count)
    target = term_target.reshape(item_count)
    whole_psi = lax.all_gather(wavefunction, "term", axis=1, tiled=True)
    selected_blocks = jnp.take(whole_psi, source, axis=0)
    half_products = jnp.einsum(
        "xwm,xmp->xwp", left_operator_blocks, selected_blocks, preferred_element_type=F32
    )
    half_products = half_products.astype(BF16)
    term_products = jnp.einsum(
        "iab,icb->iac", half_products, right_blocks, preferred_element_type=F32
    )
    onehot = (target[:, None] == jnp.arange(sectors, dtype=jnp.int32)[None, :]).astype(F32)
    partial_value = jnp.einsum(
        "is,iac->sac", onehot, term_products, precision=lax.Precision.HIGHEST
    )
    column_share = lax.psum_scatter(partial_value, "blk", scatter_dimension=2, tiled=True)
    both_share = lax.psum_scatter(column_share, "term", scatter_dimension=1, tiled=True)
    applied = lax.all_gather(both_share, "blk", axis=2, tiled=True)
    wave_float = wavefunction.astype(F32)
    correlation, norm_squared = lax.psum(
        (jnp.sum(wave_float * applied), jnp.sum(wave_float * wave_float)), "term"
    )
    rayleigh = correlation / (norm_squared + 1e-06)
    residual = applied - rayleigh * wave_float
    return (applied, residual)


def solution(mesh):
    n, groups = mesh.shape["term"], mesh.shape["blk"]

    def local(wavefunction, *rest):
        sectors, rows, _ = wavefunction.shape
        if groups == sectors == 4 and n == 4 and rows % 16 == 0:
            return fused(wavefunction, *rest, n)
        return plain(wavefunction, *rest)

    return jax.shard_map(
        local,
        mesh=mesh,
        in_specs=(
            P("parts", "term", None),
            P(("parts", "term", "blk"), None, None, None),
            P(("parts", "term", "blk"), None, None, None),
            P(("parts", "term", "blk"), None),
            P(("parts", "term", "blk"), None),
        ),
        out_specs=(P("parts", "term", None), P("parts", "term", None)),
        check_vma=False,
    )
```
